32 devices in a mesh: row: 4 (over y, core), col: 8 (over z, x).
Axes of the slice: x: 2, y: 2, z: 4, core: 2. Of those that a mesh axis runs over, the one named last changes fastest.
Arguments:
- features: bfloat16 [16, 524288], P(None, ('row', 'col')), may hold values from -6 to 6
- point_weights: bfloat16 [8, 524288], P(None, ('row', 'col')), may hold values from 0.049804688 to 1
- point_corner: int32 [524288], P(('row', 'col')), may hold values from 0 to 342
- block_owner: int32 [4096, 1], P(('row', 'col')), may hold values from 0 to 31; in each aligned block of 128 rows (0 to 127, 128 to 255, ...) at most 8 rows name the same one
- block_cell: int32 [4096], P(('row', 'col')), may hold values from 0 to 1023
- spec_weight: bfloat16 [64, 64, 16, 16, 128], P('col', 'row'), may hold values from -12 to 12
- skip_weight: bfloat16 [16, 16], replicated, may hold values from -1.5 to 1.5
- mlp_in: bfloat16 [64, 16], replicated, may hold values from -1.5 to 1.5
- mlp_bias: float32 [64], replicated, may hold values from -4 to 4
- mlp_out: bfloat16 [16, 64], replicated, may hold values from -0.75 to 0.75
Outputs:
- point_values: bfloat16 [16, 524288], P(None, ('row', 'col'))
The draws below stay inside these ranges and needn't reach their ends.
Inputs may be any that keep to these rules, and one draw needn't show every extreme that they name: `block_owner`: in each aligned block of 128 rows (the point blocks of one device) no device number appears more than 8 times; devices are numbered r * 8 + s over row r and column s.
All inputs are finite; a program needn't handle non-finite values.
Results may differ from the reference program's by a relative error of at most 0.013.
Values may be sent and summed in bfloat16 or wider, within the bound.
A program may use at most 320 MiB of HBM per device.

```python
import math
import jax
import jax.numpy as jnp
import numpy as np
from jax import lax

GRID = 256
CH = 16
MODES = 64
HID = 64
BE = 8
PB_PTS = 128
PB_DEV = 128
PBLOCKS = 4096
POINTS = 524288
CAP = 8
XL = 64
YL = 32
BLK_DEV = 1024
N_COL = 8
DEVICES = 32


def place_ends(array, stream_key, smallest, top_value):
    longest = array.shape.index(max(array.shape))
    spots = []
    for shift in (0, 1):
        where = [jax.random.randint(jax.random.fold_in(stream_key, axis), (), 0, length) for axis, length in enumerate(array.shape)]
        where[longest] = (where[longest] + shift) % array.shape[longest]
        spots.append(tuple(where))
    return array.at[spots[0]].set(smallest).at[spots[1]].set(top_value)


def levels(key, extent, split, low, largest):
    level, own = 1.0, jax.random.fold_in(key, 6)
    for position, parts in split:
        draws = jnp.exp(jax.random.uniform(jax.random.fold_in(own, position), (parts,), jnp.float32, low / len(split), largest / len(split)))
        level = level * jnp.repeat(draws, extent[position] // parts).reshape([-1 if axis == position else 1 for axis in range(len(extent))])
    return level


def deal_out(own_key, own, number, rows, count, top, reach, skew):
    ranking = jax.random.permutation(own_key, count)
    heavy_load, usual = shares(count, rows * top, reach, skew, True), shares(count, rows * top, reach, skew, False)
    places = jnp.arange(count)

    def named(lengths, turn):
        used = int((lengths > 0).sum())
        fixed = max(1, used // 4)
        shifted = fixed + (places - fixed + turn * (used - fixed)) % max(1, count - fixed)
        return jnp.zeros((count,), jnp.int32).at[ranking[jnp.where(places < fixed, places, shifted)]].set(jnp.asarray(lengths, jnp.int32))

    lengths = jnp.where(number % 4 == 0, named(heavy_load, number // 4), named(usual, number - number // 4 - 1))
    mixed = jax.random.permutation(jax.random.fold_in(own, 3), count)
    donor, taker = mixed[0:count // 2 * 2:2], mixed[1:count // 2 * 2:2]
    slack = jnp.minimum(lengths[donor] - 1, reach - lengths[taker]) // 2
    slack = jnp.where((donor == ranking[0]) | (taker == ranking[0]) | (lengths[taker] == 0), 0, jnp.maximum(slack, 0))
    shifted = jax.random.randint(jax.random.fold_in(own, 4), (count // 2,), 0, 1 << 20) % (slack + 1)
    lengths = lengths.at[donor].add(-shifted).at[taker].add(shifted)
    labels = jnp.searchsorted(jnp.cumsum(lengths), jnp.arange(rows * top), side="right").astype(jnp.int32)
    table = labels.reshape(top, rows).T
    table = table[jax.random.permutation(jax.random.fold_in(own, 1), rows)]
    turn = jax.random.randint(jax.random.fold_in(own, 2), (rows, 1), 0, top)
    return jnp.take_along_axis(table, (jnp.arange(top)[None, :] + turn) % top, axis=1)


def shares(amount, total, limit, slope, full):
    loads = [(1 << 20) // math.isqrt(rank ** slope) + 1 for rank in range(1, amount + 1)]
    largest = limit if full else min(limit, max(-(-total // amount), total * loads[0] // sum(loads)))
    least = 1 if total - largest >= amount - 1 else 0
    holding, spare = [largest] + [least] * (amount - 1), total - largest - least * (amount - 1)
    while spare > 0:
        movable = [i for i in range(1, amount) if holding[i] < largest] or [i for i in range(1, amount) if holding[i] < limit]
        whole, remaining = sum([loads[i] for i in movable]), spare
        for i in movable:
            more = min(limit - holding[i], max(1, remaining * loads[i] // whole), spare)
            holding[i] = holding[i] + more
            spare = spare - more
    return np.array(holding)


def bell_draw(stream_key, dims, deviation, most, split=(), held_as=jnp.bfloat16):
    result = jax.random.normal(stream_key, dims, jnp.float32) * deviation
    if len(split) > 0:
        result = levels(stream_key, dims, split, -0.22, 0.18) * result
    return jnp.clip(result, min=-most, max=most).astype(held_as)


def setup_inputs(seed: int = 0) -> dict:
    key_list = jax.random.split(jax.random.key(seed), 11)
    features = bell_draw(key_list[0], (CH, POINTS), 1.0, 6.0, ((1, 32),))
    point_weights = jnp.clip(0.049804688 + 0.9501953 * jax.random.uniform(key_list[1], (8, POINTS), jnp.float32) ** levels(key_list[1], (8, POINTS), ((1, 32),), -0.2, 0.2), 0.049804688, 1.0).astype(jnp.bfloat16)
    point_corner = place_ends(jax.random.randint(key_list[2], (POINTS,), 0, (BE - 1)**3), jax.random.fold_in(key_list[2], 1), 0, ((BE - 1)**3) - 1).astype(jnp.int32)
    block_owner_keys = jax.random.split(jax.random.fold_in(key_list[3], 1), PBLOCKS // PB_DEV)
    block_owner_turns = jax.random.permutation(jax.random.fold_in(key_list[3], 3), PBLOCKS // PB_DEV)
    block_owner = jax.vmap(lambda own, number: deal_out(jax.random.fold_in(key_list[3], 2), own, number, PB_DEV, DEVICES, 1, CAP, 2))(block_owner_keys, block_owner_turns).reshape((PBLOCKS, 1))
    block_cell = place_ends(jax.random.randint(key_list[4], (PBLOCKS,), 0, BLK_DEV), jax.random.fold_in(key_list[4], 1), 0, BLK_DEV - 1).astype(jnp.int32)
    spec_weight = bell_draw(key_list[5], (MODES, MODES, CH, CH, 2 * MODES), 2.0, 12.0, ((0, 8), (1, 4)))
    skip_weight = bell_draw(key_list[6], (CH, CH), CH ** -0.5, 1.5)
    mlp_in = bell_draw(key_list[7], (HID, CH), CH ** -0.5, 1.5)
    mlp_bias = bell_draw(key_list[8], (HID,), 1.0, 4.0, (), jnp.float32)
    mlp_out = bell_draw(key_list[9], (CH, HID), HID ** -0.5, 0.75)
    return {"features": features, "point_weights": point_weights, "point_corner": point_corner, "block_owner": block_owner, "block_cell": block_cell, "spec_weight": spec_weight, "skip_weight": skip_weight, "mlp_in": mlp_in, "mlp_bias": mlp_bias, "mlp_out": mlp_out}


def frequencies(count, length):
    index = jnp.arange(count, dtype=jnp.int32)
    return jnp.where(index < count // 2, index, length - count + index)

def angles(length, freq):
    places = jnp.arange(length, dtype=jnp.int32)
    turns = places[:, None] * freq[None, :] % length
    return 2.0 * math.pi / length * turns.astype(jnp.float32)

def forward_tables(length, count):
    factor = 1.0 / math.sqrt(length)
    theta = angles(length, jnp.arange(count, dtype=jnp.int32))
    real_basis_table = jnp.stack([jnp.cos(theta) * factor, -jnp.sin(theta) * factor], -1).reshape(length, 2 * count)
    theta = angles(length, frequencies(count, length))
    cosine = jnp.cos(theta) * factor
    sine = jnp.sin(theta) * factor
    from_real = jnp.stack([cosine, -sine], -1)
    from_imag = jnp.stack([sine, cosine], -1)
    paired = jnp.stack([from_real, from_imag], 0)
    planar = jnp.swapaxes(paired, 2, 3)
    return (real_basis_table.astype(jnp.bfloat16), paired.reshape(2, length, 2 * count).astype(jnp.bfloat16), planar.reshape(2, length, 2 * count).astype(jnp.bfloat16))

def inverse_tables(length, count):
    factor = 1.0 / math.sqrt(length)
    theta = angles(length, frequencies(count, length)).T
    cosine = jnp.cos(theta) * factor
    sine = jnp.sin(theta) * factor
    from_real = jnp.stack([cosine, sine], 1)
    from_imag = jnp.stack([-sine, cosine], 1)
    paired = jnp.stack([from_real, from_imag], 1)
    planar = jnp.swapaxes(paired, 0, 1)
    theta = angles(length, jnp.arange(count, dtype=jnp.int32)).T
    double = jnp.where(jnp.arange(count) == 0, 1.0, 2.0).astype(jnp.float32)[:, None]
    real_out = jnp.stack([double * jnp.cos(theta) * factor, -double * jnp.sin(theta) * factor], 1)
    return (real_out.reshape(2 * count, length).astype(jnp.bfloat16), paired.reshape(2 * count, 2, length).astype(jnp.bfloat16), planar.reshape(2 * count, 2, length).astype(jnp.bfloat16))

def corner_cell_indices(point_corner, edge_len):
    interior = edge_len - 1
    anchor = point_corner // (interior * interior) * edge_len * edge_len
    anchor = anchor + point_corner // interior % interior * edge_len + point_corner % interior
    corners = jnp.arange(8, dtype=jnp.int32)
    offsets = corners // 4 * edge_len * edge_len + corners // 2 % 2 * edge_len + corners % 2
    return (anchor[None, :] + offsets[:, None]).astype(jnp.int32)

def mix_modes(spectrum, weight):
    half = weight.shape[-1] // 2
    value_entries = spectrum.astype(jnp.float32)
    coeffs = weight.astype(jnp.float32)
    swapped = jnp.concatenate([value_entries[..., half:], value_entries[..., :half]], -1)
    real_part = jnp.concatenate([coeffs[..., :half], coeffs[..., :half]], -1)
    imag_part = jnp.concatenate([-coeffs[..., half:], coeffs[..., half:]], -1)
    total = value_entries[..., :, None, :] * real_part + swapped[..., :, None, :] * imag_part
    return lax.optimization_barrier(jnp.sum(total, axis=-3)).astype(jnp.bfloat16)

def reference(features, point_weights, point_corner, block_owner, block_cell, spec_weight, skip_weight, mlp_in, mlp_bias, mlp_out):
    block_cells = BE ** 3
    y_blocks = YL // BE
    z_blocks = GRID // BE
    owner = block_owner[:, 0]
    row_index = owner // N_COL
    col_index = owner % N_COL
    block_x = block_cell // (y_blocks * z_blocks)
    block_y = block_cell // z_blocks % y_blocks
    block_z = block_cell % z_blocks
    lanes = jnp.arange(block_cells, dtype=jnp.int32)
    cell_x = (row_index * XL + block_x * BE)[:, None] + (lanes // (BE * BE))[None, :]
    cell_y = (col_index * YL + block_y * BE)[:, None] + (lanes // BE % BE)[None, :]
    cell_z = (block_z * BE)[:, None] + (lanes % BE)[None, :]
    global_index = ((cell_x * GRID + cell_y) * GRID + cell_z).astype(jnp.int32)
    corner_cell = corner_cell_indices(point_corner, BE)
    point_block = (jnp.arange(POINTS, dtype=jnp.int32) // PB_PTS).astype(jnp.int32)
    segment_ids = (point_block[None, :] * block_cells + corner_cell).astype(jnp.int32)
    weights_f = point_weights.astype(jnp.float32)

    def scatter_channel(feature_row):
        value_entries = feature_row.astype(jnp.float32)[None, :] * weights_f
        partial_value = jax.ops.segment_sum(value_entries.reshape(-1), segment_ids.reshape(-1), num_segments=PBLOCKS * block_cells)
        partial_value = lax.optimization_barrier(partial_value.astype(jnp.bfloat16)).astype(jnp.float32)
        field = jnp.zeros((GRID ** 3,), jnp.float32).at[global_index.reshape(-1)].add(partial_value)
        return field.astype(jnp.bfloat16)
    grid = lax.map(scatter_channel, features)
    table_z, table_y, table_x = forward_tables(GRID, MODES)
    inv_z, inv_y, inv_x = inverse_tables(GRID, MODES)

    def forward(field):
        field = field.reshape(GRID * GRID, GRID)
        zspec = jnp.dot(field, table_z, preferred_element_type=jnp.float32).astype(jnp.bfloat16)
        moved = zspec.reshape(GRID, GRID, MODES, 2).transpose(0, 2, 3, 1).reshape(GRID * MODES, 2 * GRID)
        yspec = jnp.dot(moved, table_y.reshape(2 * GRID, 2 * MODES), preferred_element_type=jnp.float32).astype(jnp.bfloat16)
        moved = yspec.reshape(GRID, MODES, MODES, 2).transpose(1, 2, 3, 0).reshape(MODES * MODES, 2 * GRID)
        spec = jnp.dot(moved, table_x.reshape(2 * GRID, 2 * MODES), preferred_element_type=jnp.float32).astype(jnp.bfloat16)
        return spec.reshape(MODES, MODES, 2 * MODES)
    spectrum = lax.map(forward, grid)
    by_kz = spectrum.transpose(1, 2, 0, 3)

    def mix_slice(pair):
        return mix_modes(pair[0], pair[1])
    mixed = lax.map(mix_slice, (by_kz, spec_weight))
    mixed = mixed.transpose(2, 0, 1, 3)

    def inverse_xy(modes):
        xinv = jnp.dot(modes.reshape(MODES * MODES, 2 * MODES), inv_x.reshape(2 * MODES, 2 * GRID), preferred_element_type=jnp.float32).astype(jnp.bfloat16)
        moved = xinv.reshape(MODES, MODES, 2, GRID).transpose(0, 3, 1, 2).reshape(MODES * GRID, 2 * MODES)
        yinv = jnp.dot(moved, inv_y.reshape(2 * MODES, 2 * GRID), preferred_element_type=jnp.float32).astype(jnp.bfloat16)
        return yinv.reshape(MODES, GRID, 2, GRID)
    section = lax.map(inverse_xy, mixed)
    slab_len = 2
    slab_count = GRID // slab_len
    section_slabs = jnp.moveaxis(section.reshape(CH, MODES, slab_count, slab_len, 2, GRID), 2, 0)
    grid_slabs = jnp.moveaxis(grid.reshape(CH, slab_count, slab_len, GRID, GRID), 1, 0)
    inv_z_f = inv_z.astype(jnp.float32).reshape(MODES, 2, GRID)
    skip_f = skip_weight.astype(jnp.float32)
    first_f = mlp_in.astype(jnp.float32)
    second_f = mlp_out.astype(jnp.float32)
    high = lax.Precision.HIGHEST

    def layer_grid_plane(pair):
        modes, field = pair
        spectral = jnp.einsum('okxpy,kpz->oxyz', modes.astype(jnp.float32), inv_z_f, precision=high)
        pre = spectral + jnp.einsum('oi,ixyz->oxyz', skip_f, field.astype(jnp.float32), precision=high)
        pre = pre.astype(jnp.bfloat16).astype(jnp.float32)
        hidden = jnp.einsum('hi,ixyz->hxyz', first_f, pre, precision=high) + mlp_bias[:, None, None, None]
        hidden = jax.nn.gelu(hidden).astype(jnp.bfloat16).astype(jnp.float32)
        return jnp.einsum('oh,hxyz->oxyz', second_f, hidden, precision=high).astype(jnp.bfloat16)
    layer_grid = lax.map(layer_grid_plane, (section_slabs, grid_slabs))
    layer_grid = jnp.moveaxis(layer_grid, 0, 1).reshape(CH, GRID ** 3)
    point_index = global_index[point_block[None, :], corner_cell]

    def interpolate(field):
        picked = field[point_index].astype(jnp.float32)
        return lax.optimization_barrier(jnp.sum(picked * weights_f, axis=0)).astype(jnp.bfloat16)
    return lax.map(interpolate, layer_grid)
```

```python
import functools
import math

import jax
import jax.numpy as jnp
from jax import lax
from jax.experimental import pallas as pl
from jax.experimental.pallas import tpu as pltpu
from jax.sharding import PartitionSpec as P

GRID = 256
BE = 8
PB_PTS = 128


def frequencies(count, length):
    index = jnp.arange(count, dtype=jnp.int32)
    return jnp.where(index < count // 2, index, length - count + index)


def angles(length, freq):
    places = jnp.arange(length, dtype=jnp.int32)
    turns = places[:, None] * freq[None, :] % length
    return 2.0 * math.pi / length * turns.astype(jnp.float32)


def forward_tables(length, count):
    factor = 1.0 / math.sqrt(length)
    theta = angles(length, jnp.arange(count, dtype=jnp.int32))
    real_basis_table = jnp.stack([jnp.cos(theta) * factor, -jnp.sin(theta) * factor], -1).reshape(
        length, 2 * count
    )
    theta = angles(length, frequencies(count, length))
    cosine = jnp.cos(theta) * factor
    sine = jnp.sin(theta) * factor
    from_real = jnp.stack([cosine, -sine], -1)
    from_imag = jnp.stack([sine, cosine], -1)
    paired = jnp.stack([from_real, from_imag], 0)
    planar = jnp.swapaxes(paired, 2, 3)
    return (
        real_basis_table.astype(jnp.bfloat16),
        paired.reshape(2, length, 2 * count).astype(jnp.bfloat16),
        planar.reshape(2, length, 2 * count).astype(jnp.bfloat16),
    )


def inverse_tables(length, count):
    factor = 1.0 / math.sqrt(length)
    theta = angles(length, frequencies(count, length)).T
    cosine = jnp.cos(theta) * factor
    sine = jnp.sin(theta) * factor
    from_real = jnp.stack([cosine, sine], 1)
    from_imag = jnp.stack([-sine, cosine], 1)
    paired = jnp.stack([from_real, from_imag], 1)
    planar = jnp.swapaxes(paired, 0, 1)
    theta = angles(length, jnp.arange(count, dtype=jnp.int32)).T
    double = jnp.where(jnp.arange(count) == 0, 1.0, 2.0).astype(jnp.float32)[:, None]
    real_out = jnp.stack([double * jnp.cos(theta) * factor, -double * jnp.sin(theta) * factor], 1)
    return (
        real_out.reshape(2 * count, length).astype(jnp.bfloat16),
        paired.reshape(2 * count, 2, length).astype(jnp.bfloat16),
        planar.reshape(2 * count, 2, length).astype(jnp.bfloat16),
    )


BF = jnp.bfloat16
F32 = jnp.float32
CORNERS = 8
VMEM_BYTES = 48 * 1024 * 1024


def vmem(limit=VMEM_BYTES):
    return pltpu.CompilerParams(vmem_limit_bytes=limit)


def block_masks(rows, channels):
    edge = BE
    base = channels + CORNERS
    vx, vy, vz = rows[base : base + 1], rows[base + 1 : base + 2], rows[base + 2 : base + 3]
    place = lax.broadcasted_iota(jnp.int32, (edge, PB_PTS), 0).astype(F32)
    plane = lax.broadcasted_iota(jnp.int32, (edge, edge, PB_PTS), 0).astype(F32)
    z_low, z_high = place == vz, place == vz + 1.0
    y_low, y_high = plane == vy[None], plane == (vy + 1.0)[None]
    parts = []
    for dx in range(2):
        lines = []
        for dy in range(2):
            k = channels + dx * 4 + dy * 2
            lines.append(
                jnp.where(z_low, rows[k : k + 1], jnp.where(z_high, rows[k + 1 : k + 2], 0.0))
            )
        face = jnp.where(y_low, lines[0][None], jnp.where(y_high, lines[1][None], 0.0))
        parts.append(face.reshape(edge * edge, PB_PTS))
    spread = jnp.concatenate(parts, axis=1).astype(BF)
    return spread, place == vx, place == vx + 1.0


def spread_kernel(channels, recv_ref, out_ref):
    for s in range(recv_ref.shape[0]):
        rows = recv_ref[s].astype(F32)
        spread, x_low, x_high = block_masks(rows, channels)
        feats = rows[:channels][:, None, :]
        low = jnp.where(x_low[None], feats, 0.0).reshape(channels * BE, PB_PTS)
        high = jnp.where(x_high[None], feats, 0.0).reshape(channels * BE, PB_PTS)
        both = jnp.concatenate([low, high], axis=1).astype(BF)
        out_ref[s] = lax.dot_general(
            spread, both, (((1,), (1,)), ((), ())), preferred_element_type=F32
        ).astype(BF)


def land_kernel(
    y_blocks, x_blocks, z_blocks, id_row, id_col, blocks_ref, table_ref, out_ref, own_ref, land, grid
):
    slots = id_row.shape[1]
    local = land.shape[0]
    lanes = blocks_ref.shape[-1]
    parts = out_ref.shape[0]

    @pl.when(pl.program_id(0) == 0)
    def _():
        cells = lax.broadcasted_iota(jnp.int32, (local, slots), 0) + 1
        land[...] = jnp.where(cells == id_row[...], 1.0, 0.0).astype(BF)

    same = jnp.where(id_col[...] == id_row[...], 1.0, 0.0).astype(BF)
    for dz in range(BE):
        piece = blocks_ref[0, dz]
        grid[dz] = jnp.dot(land[...], piece, preferred_element_type=F32).astype(BF)
        own_ref[0, dz] = jnp.dot(same, piece, preferred_element_type=F32).astype(BF)
    for bx in range(x_blocks):
        for by in range(y_blocks):
            start = (bx * y_blocks + by) * z_blocks
            column = grid[:, start : start + z_blocks, :].reshape(BE * z_blocks, lanes)
            got = jnp.dot(table_ref[...], column, preferred_element_type=F32).astype(BF)
            out_ref[:, by, 0, :, bx * lanes : (bx + 1) * lanes] = got.reshape(
                parts, got.shape[0] // parts, lanes
            )


def mix_kernel(spec_ref, weight_ref, out_ref):
    half = spec_ref.shape[-1] // 2
    channels = spec_ref.shape[2]
    first = lax.broadcasted_iota(jnp.int32, weight_ref.shape[-2:], 1) < half

    def step(j, carry):
        value = spec_ref[0, pl.ds(j, 1)][0]
        turned = pltpu.roll(value, half, 1)
        total = jnp.zeros(weight_ref.shape[-2:], F32)
        for c in range(channels):
            w = weight_ref[0, pl.ds(j, 1), c][0].astype(F32)
            other = pltpu.roll(w, half, 1)
            real = jnp.where(first, w, other)
            imag = jnp.where(first, -other, w)
            total = total + value[c : c + 1] * real + turned[c : c + 1] * imag
        out_ref[0, pl.ds(j, 1)] = total.astype(BF)[None]
        return carry

    lax.fori_loop(0, spec_ref.shape[1], step, 0)


def back_kernel(z_blocks, in_ref, table_ref, out_ref):
    lanes = out_ref.shape[-1]
    for dy in range(BE):
        modes = in_ref[:, dy, :, :].reshape(table_ref.shape[1], lanes)
        got = jnp.dot(table_ref[...], modes, preferred_element_type=F32)
        out_ref[0, :, dy * BE : (dy + 1) * BE, :] = got.reshape(z_blocks, BE, lanes)


def point_kernel(channels, recv_ref, spec_ref, own_ref, skip_ref, in_ref, bias_ref, last_ref, out_ref):
    group, cells, lanes = spec_ref.shape
    own = own_ref[...].reshape(group * cells, lanes)
    pre = spec_ref[...].reshape(group * cells, lanes) + jnp.dot(
        own, skip_ref[...], preferred_element_type=F32
    )
    hidden = jnp.dot(pre.astype(BF), in_ref[...], preferred_element_type=F32) + bias_ref[...]
    hidden = jax.nn.gelu(hidden, approximate=True).astype(BF)
    layer = jnp.dot(hidden, last_ref[...], preferred_element_type=F32).astype(BF)
    layer = layer.reshape(group, cells, lanes)
    for s in range(group):
        rows = recv_ref[s].astype(F32)
        spread, x_low, x_high = block_masks(rows, channels)
        picked = lax.dot_general(
            layer[s], spread, (((0,), (0,)), ((), ())), preferred_element_type=F32
        )
        low = picked[:, :PB_PTS].reshape(channels, BE, PB_PTS)
        high = picked[:, PB_PTS:].reshape(channels, BE, PB_PTS)
        total = jnp.where(x_low[None], low, 0.0) + jnp.where(x_high[None], high, 0.0)
        out_ref[s] = jnp.sum(total, axis=1).astype(BF)


def whole_spec(shape):
    return pl.BlockSpec(shape, lambda *_: (0,) * len(shape))


def body(
    features,
    point_weights,
    point_corner,
    block_owner,
    block_cell,
    spec_weight,
    skip_weight,
    mlp_in,
    mlp_bias,
    mlp_out,
):
    row_count = lax.axis_size("row")
    col_count = lax.axis_size("col")
    devices = row_count * col_count
    channels = features.shape[0]
    block_count = block_cell.shape[0]
    edge_len = BE
    cells = edge_len * edge_len
    lanes = channels * edge_len
    grid_len = GRID
    mode_count = spec_weight.shape[-1] // 2
    hid = mlp_in.shape[0]
    capacity = max(2, (2 * block_count + devices - 1) // devices)
    slots = devices * capacity
    x_local = grid_len // row_count
    y_local = grid_len // col_count
    x_blocks = x_local // edge_len
    y_blocks = y_local // edge_len
    z_blocks = grid_len // edge_len
    local_blocks = x_blocks * y_blocks * z_blocks
    wide = x_blocks * lanes
    owner = block_owner[:, 0]
    block_ids = jnp.arange(block_count, dtype=jnp.int32)
    earlier = block_ids[None, :] < block_ids[:, None]
    rank = jnp.sum((owner[None, :] == owner[:, None]) & earlier, axis=1)
    slot = owner * capacity + rank
    slot_ids = jnp.arange(slots, dtype=jnp.int32)
    match = slot[None, :] == slot_ids[:, None]
    filled = jnp.any(match, axis=1)
    block_of_slot = jnp.sum(jnp.where(match, block_ids[None, :], 0), axis=1)
    interior = edge_len - 1
    corner = point_corner.reshape(block_count, PB_PTS)
    code = (block_cell + 1)[:, None] + jnp.zeros((1, PB_PTS), jnp.int32)
    extra = [
        corner // (interior * interior),
        corner // interior % interior,
        corner % interior,
        code // 32,
        code % 32,
    ]
    used = channels + CORNERS + len(extra)
    rows_sent = (used + 15) // 16 * 16
    extra = extra + [jnp.zeros_like(corner)] * (rows_sent - used)
    payload = jnp.concatenate(
        [
            features.reshape(channels, block_count, PB_PTS),
            point_weights.reshape(CORNERS, block_count, PB_PTS),
            jnp.stack(extra, 0).astype(BF),
        ],
        axis=0,
    ).transpose(1, 0, 2)
    sent = jnp.where(filled[:, None, None], payload[block_of_slot], jnp.zeros((), BF))
    recv = lax.all_to_all(sent, ("row", "col"), split_axis=0, concat_axis=0, tiled=True)
    id_at = channels + CORNERS + 3
    ids = recv[:, id_at, 0].astype(jnp.int32) * 32 + recv[:, id_at + 1, 0].astype(jnp.int32)
    group = 8
    recv_spec = pl.BlockSpec((group, rows_sent, PB_PTS), lambda g: (g, 0, 0))
    cell_spec = pl.BlockSpec((group, cells, lanes), lambda g: (g, 0, 0))
    blocks = pl.pallas_call(
        functools.partial(spread_kernel, channels),
        out_shape=jax.ShapeDtypeStruct((slots, cells, lanes), BF),
        grid=(slots // group,),
        in_specs=[recv_spec],
        out_specs=cell_spec,
        compiler_params=vmem(),
        name="spread",
    )(recv)
    by_cell = blocks.transpose(1, 0, 2).reshape(edge_len, edge_len, slots, lanes)
    table_z, table_y, table_x = forward_tables(grid_len, mode_count)
    inv_z, inv_y, inv_x = inverse_tables(grid_len, mode_count)
    z_table = (
        table_z.reshape(z_blocks, edge_len, 2 * mode_count)
        .transpose(2, 1, 0)
        .reshape(2 * mode_count, grid_len)
    )
    modes_out = 2 * mode_count // col_count
    zspec, own = pl.pallas_call(
        functools.partial(land_kernel, y_blocks, x_blocks, z_blocks),
        out_shape=(
            jax.ShapeDtypeStruct((col_count, y_blocks, edge_len, modes_out, wide), BF),
            jax.ShapeDtypeStruct((edge_len, edge_len, slots, lanes), BF),
        ),
        grid=(edge_len,),
        in_specs=[
            whole_spec((1, slots)),
            whole_spec((slots, 1)),
            pl.BlockSpec((1, edge_len, slots, lanes), lambda d: (d, 0, 0, 0)),
            whole_spec((2 * mode_count, grid_len)),
        ],
        out_specs=(
            pl.BlockSpec((col_count, y_blocks, 1, modes_out, wide), lambda d: (0, 0, d, 0, 0)),
            pl.BlockSpec((1, edge_len, slots, lanes), lambda d: (d, 0, 0, 0)),
        ),
        scratch_shapes=[
            pltpu.VMEM((local_blocks, slots), BF),
            pltpu.VMEM((edge_len, local_blocks, lanes), BF),
        ],
        compiler_params=vmem(),
        name="land",
    )(ids[None, :], ids[:, None], by_cell, z_table)
    own = own.reshape(cells, slots, lanes).transpose(1, 0, 2)
    zspec = lax.all_to_all(zspec, "col", split_axis=0, concat_axis=0, tiled=True)
    kz_local = modes_out // 2
    zspec = zspec.reshape(grid_len, modes_out, wide).transpose(1, 0, 2)
    yspec = jnp.einsum(
        "krn,rq->kqn",
        zspec.reshape(kz_local, 2 * grid_len, wide),
        table_y.reshape(2 * grid_len, 2 * mode_count),
        preferred_element_type=F32,
    ).astype(BF)
    spots = jnp.arange(wide, dtype=jnp.int32)
    channel = spots // edge_len % channels
    target = channel * x_local + spots // lanes * edge_len + spots % edge_len
    order = (target[:, None] == spots[None, :]).astype(BF)
    yspec = jnp.einsum("kqn,nm->kqm", yspec, order, preferred_element_type=F32).astype(BF)
    yspec = yspec.reshape(kz_local, 2 * mode_count, channels, x_local)
    yspec = lax.all_to_all(yspec, "row", split_axis=1, concat_axis=3, tiled=True)
    ky_local = yspec.shape[1] // 2
    spectrum = jnp.einsum(
        "kjpcx,pxq->kjcq",
        yspec.reshape(kz_local, ky_local, 2, channels, grid_len),
        table_x,
        preferred_element_type=F32,
    ).astype(BF).astype(F32)
    mode_spec = pl.BlockSpec((1, ky_local, channels, 2 * mode_count), lambda k: (k, 0, 0, 0))
    mixed = pl.pallas_call(
        mix_kernel,
        out_shape=jax.ShapeDtypeStruct(spectrum.shape, BF),
        grid=(kz_local,),
        in_specs=[
            mode_spec,
            pl.BlockSpec((1,) + spec_weight.shape[1:], lambda k: (k, 0, 0, 0, 0)),
        ],
        out_specs=mode_spec,
        compiler_params=vmem(),
        name="mix",
    )(spectrum, spec_weight)
    xinv = jnp.einsum("kjoq,qpx->kjpox", mixed, inv_x, preferred_element_type=F32).astype(BF)
    xinv = xinv.reshape(kz_local, 2 * ky_local, channels, grid_len)
    xinv = lax.all_to_all(xinv, "row", split_axis=3, concat_axis=1, tiled=True)
    xinv = xinv.reshape(kz_local, 2 * mode_count, wide)
    xinv = jnp.einsum("kqm,nm->kqn", xinv, order, preferred_element_type=F32).astype(BF)
    yinv = jnp.einsum(
        "rq,kqn->krn",
        inv_y.reshape(2 * mode_count, 2 * grid_len).T,
        xinv,
        preferred_element_type=F32,
    ).astype(BF)
    yinv = yinv.reshape(modes_out, grid_len, wide).transpose(1, 0, 2)
    yinv = lax.all_to_all(yinv, "col", split_axis=0, concat_axis=0, tiled=True)
    yinv = yinv.reshape(col_count, y_local, modes_out, wide)
    spectral = pl.pallas_call(
        functools.partial(back_kernel, z_blocks),
        out_shape=jax.ShapeDtypeStruct((x_blocks * y_blocks, z_blocks, cells, lanes), F32),
        grid=(x_blocks, y_blocks),
        in_specs=[
            pl.BlockSpec(
                (col_count, edge_len, modes_out, lanes), lambda bx, by: (0, by, 0, bx)
            ),
            whole_spec((grid_len, 2 * mode_count)),
        ],
        out_specs=pl.BlockSpec(
            (1, z_blocks, cells, lanes), lambda bx, by: (bx * y_blocks + by, 0, 0, 0)
        ),
        compiler_params=vmem(),
        name="back",
    )(yinv, inv_z.T)
    spectral = spectral.reshape(local_blocks, cells, lanes)[jnp.maximum(ids - 1, 0)]
    eye = jnp.eye(edge_len, dtype=BF)
    values = pl.pallas_call(
        functools.partial(point_kernel, channels),
        out_shape=jax.ShapeDtypeStruct((slots, channels, PB_PTS), BF),
        grid=(slots // group,),
        in_specs=[
            recv_spec,
            cell_spec,
            cell_spec,
            whole_spec((lanes, lanes)),
            whole_spec((lanes, hid * edge_len)),
            whole_spec((1, hid * edge_len)),
            whole_spec((hid * edge_len, lanes)),
        ],
        out_specs=pl.BlockSpec((group, channels, PB_PTS), lambda g: (g, 0, 0)),
        compiler_params=vmem(),
        name="points",
    )(
        recv,
        spectral,
        own,
        jnp.kron(skip_weight.T, eye),
        jnp.kron(mlp_in.T, eye),
        jnp.repeat(mlp_bias, edge_len)[None, :],
        jnp.kron(mlp_out.T, eye),
    )
    returned = lax.all_to_all(values, ("row", "col"), split_axis=0, concat_axis=0, tiled=True)
    points = returned[slot]
    return points.transpose(1, 0, 2).reshape(channels, block_count * PB_PTS)


def solution(mesh):
    return jax.shard_map(
        body,
        mesh=mesh,
        in_specs=(
            P(None, ("row", "col")),
            P(None, ("row", "col")),
            P(("row", "col")),
            P(("row", "col"), None),
            P(("row", "col")),
            P("col", "row", None, None, None),
            P(),
            P(),
            P(),
            P(),
        ),
        out_specs=P(None, ("row", "col")),
        check_vma=False,
    )
```
